32 devices in a mesh: tm: 32 (over z, y, x, core), band: 1, fsdp: 1.
Axes of the slice: x: 2, y: 2, z: 4, core: 2. Of those that a mesh axis runs over, the one named last changes fastest.
Arguments:
- video: bfloat16 [128, 16, 32, 256], P('tm', 'band', 'fsdp'), may hold values from -8 to 8
- clip_lengths: int32 [16], replicated, may hold values from 1 to 31, 128 in all
- norm_gains: float32 [2, 256], replicated, may hold values from 0.1 to 1.9
- spatial_kernel_weight: bfloat16 [256, 2304], P(('band', 'fsdp')), may hold values from -0.125 to 0.125
- w_time: bfloat16 [256, 768], P(('band', 'fsdp')), may hold values from -0.21875 to 0.21875
- w_qkv: bfloat16 [256, 768], P(('band', 'fsdp')), may hold values from -4 to 4
- w_out: bfloat16 [256, 256], P(('band', 'fsdp')), may hold values from -0.375 to 0.375
Outputs:
- mixed: bfloat16 [1, 1, 512, 128, 256], P('band', 'fsdp', 'tm')
The draws below stay inside these ranges and needn't reach their ends.
Inputs may be any that keep to these rules, and one draw needn't show every extreme that they name: `clip_lengths`: every clip has at least one frame and the lengths sum to 128.
All inputs are finite; a program needn't handle non-finite values.
Results may differ from the reference program's by a relative error of at most 0.0064.
Values may be sent and summed in bfloat16 or wider, within the bound.
A program may use at most 64 MiB of HBM per device.

```python
import math
import jax
import jax.numpy as jnp
import numpy as np
from jax import lax

C = 256
GROUPS = 32
ROWS_DEV = 16
COLUMNS_PER_SHARD = 32
FRAMES = 128
H = 16
W = 32
NCLIPS = 16
MOSTLEN = 31
BANDS = 1
COLBLK = 1


def draw_video(key, part):
    key_base = jax.random.fold_in(key, 11)
    key_rough = jax.random.fold_in(key, 12)
    key_level = jax.random.fold_in(key, 13)
    key_offset = jax.random.fold_in(key, 14)
    cell_rows = ROWS_DEV // 2
    cell_cols = COLUMNS_PER_SHARD // 2
    grid_rows = H // cell_rows
    grid_cols = W // cell_cols
    level = jnp.exp(jax.random.uniform(key_level, (FRAMES, grid_rows, grid_cols, 1), jnp.float32, -1.15, 1.15))
    level = jnp.repeat(jnp.repeat(level, cell_rows, axis=1), cell_cols, axis=2)
    offset = jax.random.uniform(key_offset, (FRAMES, grid_rows, grid_cols, GROUPS), jnp.float32, -0.6, 0.6)
    offset = jnp.repeat(jnp.repeat(jnp.repeat(offset, cell_rows, axis=1), cell_cols, axis=2), C // GROUPS, axis=3)
    rough = jax.random.uniform(key_rough, (FRAMES, H, W, 1), jnp.float32, 0.7, 1.3)
    base = jax.random.normal(key_base, (FRAMES, H, W, C), jnp.float32)
    whole = (0.8 * base * rough + offset) * level
    return jnp.clip(whole, -8.0, 8.0).astype(jnp.bfloat16)


def draw_w_qkv(key, part):
    scale = 1.0 / jnp.sqrt(jnp.float32(C))
    keys_part = jax.random.normal(jax.random.fold_in(key, 21), (C, C), jnp.float32) * scale
    values_part = jax.random.normal(jax.random.fold_in(key, 22), (C, C), jnp.float32) * scale
    noise = jax.random.normal(jax.random.fold_in(key, 23), (C, C), jnp.float32) * scale
    query_part = noise
    whole = jnp.concatenate([query_part, keys_part, values_part], axis=1)
    return jnp.clip(whole, -4.0, 4.0).astype(jnp.bfloat16)


def split_up(number_of, total, bound, skew):
    portions = [(1 << 20) // math.isqrt(grade ** skew) + 1 for grade in range(2, number_of + 1)]
    spare, given = total - bound - (number_of - 1), [1] * (number_of - 1)
    while spare > 0:
        candidates = [i for i in range(number_of - 1) if given[i] < bound]
        whole, left = sum([portions[i] for i in candidates]), spare
        for i in candidates:
            addition = min(bound - given[i], max(1, left * portions[i] // whole), spare)
            given[i] = given[i] + addition
            spare = spare - addition
    return np.array([bound] + given)


def ragged(own_key, amount, total, reach, slope):
    if amount == 2:
        one = jax.random.randint(own_key, (), max(1, total - reach), min(reach, total - 1) + 1)
        return jnp.stack([one, total - one])
    tallies = jnp.asarray(split_up(amount, total, reach, slope), jnp.int32)
    pairs = (amount - 1) // 2
    giver, taker = tallies[1:1 + 2 * pairs:2], tallies[2:2 + 2 * pairs:2]
    margin = jnp.minimum(giver - 1, reach - taker)
    passed = jax.random.randint(jax.random.fold_in(own_key, 1), (pairs,), 0, 1 << 20) % (margin + 1)
    tallies = tallies.at[1:1 + 2 * pairs:2].set(giver - passed).at[2:2 + 2 * pairs:2].set(taker + passed)
    return tallies[jax.random.permutation(jax.random.fold_in(own_key, 2), amount)]


def centred(key, dims, deviation, bound, kind=jnp.bfloat16):
    values = deviation * jax.random.normal(key, dims, jnp.float32)
    return jnp.clip(values, min=-bound, max=bound).astype(kind)


def setup_inputs(seed: int = 0) -> dict:
    key_list = jax.random.split(jax.random.key(seed), 8)
    return {
        "video": draw_video(jax.random.fold_in(key_list[7], 71), 0),
        "clip_lengths": ragged(key_list[1], NCLIPS, FRAMES, MOSTLEN, 1).astype(jnp.int32),
        "norm_gains": jnp.clip(1.0 + 0.18 * jax.random.normal(key_list[2], (2, C), jnp.float32), 0.1, 1.9),
        "spatial_kernel_weight": centred(key_list[3], (C, 9 * C), (9 * C) ** -0.5, 0.125),
        "w_time": centred(key_list[4], (C, 3 * C), (3 * C) ** -0.5, 0.21875),
        "w_qkv": draw_w_qkv(jax.random.fold_in(key_list[7], 71), 0),
        "w_out": centred(key_list[6], (C, C), C ** -0.5, 0.375),
    }


EPS = 1e-06

def frame_starts(clip_lengths, total):
    ends = jnp.cumsum(clip_lengths).astype(jnp.int32)
    begins = (ends - clip_lengths).astype(jnp.int32)
    index = jnp.arange(total, dtype=jnp.int32)
    chosen = jnp.where(begins[None, :] <= index[:, None], begins[None, :], 0)
    return lax.optimization_barrier(jnp.max(chosen, axis=1)).astype(jnp.int32)

def norm_frame(field, gain):
    height, width, chans = field.shape
    group_width = chans // GROUPS
    vals = field.astype(jnp.float32).reshape(height * width, GROUPS, group_width)
    count = height * width * group_width
    mean = lax.optimization_barrier(jnp.sum(vals, axis=(0, 2))) / count
    square = lax.optimization_barrier(jnp.sum(vals * vals, axis=(0, 2))) / count
    scale = lax.rsqrt(square - mean * mean + EPS)
    normed = (vals - mean[None, :, None]) * scale[None, :, None]
    return normed.reshape(height, width, chans) * gain

def space_conv(act, spatial_kernel_weight):
    height, width, chans = act.shape
    padded = jnp.pad(act, ((1, 1), (1, 1), (0, 0)))
    total = jnp.zeros((height, width, chans), jnp.float32)
    for tap in range(9):
        shift_y = tap // 3
        shift_x = tap % 3
        total = total + jnp.dot(padded[shift_y:shift_y + height, shift_x:shift_x + width], spatial_kernel_weight[:, tap * chans:(tap + 1) * chans], preferred_element_type=jnp.float32)
    return total

def reference(video, clip_lengths, norm_gains, spatial_kernel_weight, w_time, w_qkv, w_out):
    starts = frame_starts(clip_lengths, FRAMES)

    def first_section(frame):
        act = jax.nn.silu(norm_frame(frame, norm_gains[0])).astype(jnp.bfloat16)
        return space_conv(act, spatial_kernel_weight).astype(jnp.bfloat16)
    spatial = lax.map(first_section, video)

    def time_frame(index):
        total = lax.dynamic_index_in_dim(video, index, 0, keepdims=False).astype(jnp.float32)
        for tap in range(3):
            source = jnp.maximum(index - 2 + tap, starts[index]).astype(jnp.int32)
            piece = lax.dynamic_index_in_dim(spatial, source, 0, keepdims=False)
            total = total + jnp.dot(piece, w_time[:, tap * C:(tap + 1) * C], preferred_element_type=jnp.float32)
        return total.astype(jnp.bfloat16)
    resid = lax.map(time_frame, jnp.arange(FRAMES, dtype=jnp.int32))
    normed = lax.map(lambda frame: norm_frame(frame, norm_gains[1]).astype(jnp.bfloat16), resid)
    index = jnp.arange(FRAMES, dtype=jnp.int32)
    allowed = (index[None, :] <= index[:, None]) & (index[None, :] >= starts[:, None])

    def attend_query_row(row):
        rows_in = lax.dynamic_index_in_dim(normed, row, 1, keepdims=False)
        resid_row = lax.dynamic_index_in_dim(resid, row, 1, keepdims=False)
        qkv = jnp.dot(rows_in, w_qkv, preferred_element_type=jnp.float32).astype(jnp.bfloat16)
        query = qkv[..., :C].astype(jnp.float32)
        keys = qkv[..., C:2 * C].astype(jnp.float32)
        value_rows = qkv[..., 2 * C:].astype(jnp.float32)
        scores = jnp.einsum('fwc,gwc->wfg', query, keys) / math.sqrt(C)
        scores = jnp.where(allowed[None], scores, -1e+30)
        top = lax.optimization_barrier(jnp.max(scores, axis=-1, keepdims=True))
        expo = jnp.where(allowed[None], jnp.exp(scores - top), 0.0)
        attention_probabilities = (expo / lax.optimization_barrier(jnp.sum(expo, axis=-1, keepdims=True))).astype(jnp.bfloat16)
        attention_output = jnp.einsum('wfg,gwc->wfc', attention_probabilities.astype(jnp.float32), value_rows).astype(jnp.bfloat16)
        projected_output = jnp.dot(attention_output, w_out, preferred_element_type=jnp.float32)
        return (jnp.swapaxes(resid_row, 0, 1).astype(jnp.float32) + projected_output).astype(jnp.bfloat16)
    rows_out = lax.map(attend_query_row, jnp.arange(H, dtype=jnp.int32))
    blocks = rows_out.reshape(BANDS, ROWS_DEV, COLBLK, COLUMNS_PER_SHARD, FRAMES, C)
    blocks = jnp.transpose(blocks, (0, 2, 1, 3, 4, 5))
    return blocks.reshape(BANDS, COLBLK, ROWS_DEV * COLUMNS_PER_SHARD, FRAMES, C)
```

```python
import math

import jax
import jax.numpy as jnp
from jax import lax
from jax.sharding import PartitionSpec as P

GROUPS = 32


EPS = 1e-06


def with_halo(x, sides, width):
    for axis, dim in sides:
        size, length = (lax.axis_size(axis), x.shape[dim])
        up = [(i, (i + 1) % size) for i in range(size - 1)]
        down = [(j, i) for i, j in up]
        last = lax.slice_in_dim(x, length - width, length, axis=dim)
        initial = lax.slice_in_dim(x, 0, width, axis=dim)
        before = lax.ppermute(last, axis, up)
        after = lax.ppermute(initial, axis, down)
        x = jnp.concatenate([before, x, after], axis=dim)
    return x


def from_behind(x, axis, by):
    length = lax.axis_size(axis)
    pairs = [(i, i + by) for i in range(length) if 0 <= i + by < length]
    return lax.ppermute(x, axis, pairs)


def frame_starts(clip_lengths, total):
    ends = jnp.cumsum(clip_lengths)
    begins = ends - clip_lengths
    index = jnp.arange(total, dtype=jnp.int32)
    chosen = jnp.where(begins[None, :] <= index[:, None], begins[None, :], 0)
    return jnp.max(chosen, axis=1)


def group_moments(field):
    frames, height, width, chans = field.shape
    group_width = chans // GROUPS
    vals = field.astype(jnp.float32).reshape(frames, height * width, GROUPS, group_width)
    sums = jnp.sum(vals, axis=(1, 3))
    squares = jnp.sum(vals * vals, axis=(1, 3))
    sums, squares = lax.psum((sums, squares), ("band", "fsdp"))
    count = height * width * group_width * lax.axis_size("band") * lax.axis_size("fsdp")
    mean = sums / count
    scale = lax.rsqrt(squares / count - mean * mean + EPS)
    return (mean, scale)


def apply_norm(field, mean, scale, gain):
    shape = field.shape
    chans = shape[-1]
    group_width = chans // GROUPS
    vals = field.astype(jnp.float32).reshape(shape[0], -1, GROUPS, group_width)
    normed = (vals - mean[:, None, :, None]) * scale[:, None, :, None]
    return normed.reshape(shape) * gain


def body(video, clip_lengths, norm_gains, spatial_kernel_weight, w_time, w_qkv, w_out):
    space_full, time_full, qkv_full, output_complete = (
        lax.all_gather(spatial_kernel_weight, ("band", "fsdp"), axis=0, tiled=True),
        lax.all_gather(w_time, ("band", "fsdp"), axis=0, tiled=True),
        lax.all_gather(w_qkv, ("band", "fsdp"), axis=0, tiled=True),
        lax.all_gather(w_out, ("band", "fsdp"), axis=0, tiled=True),
    )
    frames, height, width, chans = video.shape
    ranks = lax.axis_size("tm")
    total_frames = frames * ranks
    first = lax.axis_index("tm") * frames
    starts = frame_starts(clip_lengths, total_frames)
    local_starts = lax.dynamic_slice_in_dim(starts, first, frames)
    mean_one, scale_one = group_moments(video)
    act = jax.nn.silu(apply_norm(video, mean_one, scale_one, norm_gains[0])).astype(jnp.bfloat16)
    padded = with_halo(act, (("band", 1), ("fsdp", 2)), 1)
    spatial = jnp.zeros((frames, height, width, chans), jnp.float32)
    for tap in range(9):
        shift_y = tap // 3
        shift_x = tap % 3
        spatial = spatial + jnp.einsum(
            "fhwc,cd->fhwd",
            padded[:, shift_y : shift_y + height, shift_x : shift_x + width],
            space_full[:, tap * chans : (tap + 1) * chans],
            preferred_element_type=jnp.float32,
        )
    spatial = spatial.astype(jnp.bfloat16)
    carried = from_behind(spatial[frames - 2 :], "tm", 1)
    extended = jnp.concatenate([carried, spatial], axis=0)
    position = first + jnp.arange(frames, dtype=jnp.int32)
    slots = jnp.arange(frames + 2, dtype=jnp.int32)
    temporal = jnp.zeros((frames, height, width, chans), jnp.float32)
    for tap in range(3):
        source = jnp.maximum(position - 2 + tap, local_starts) - first + 2
        select = (source[:, None] == slots[None, :]).astype(jnp.bfloat16)
        picked = jnp.einsum(
            "fe,ehwc->fhwc", select, extended, preferred_element_type=jnp.float32
        ).astype(jnp.bfloat16)
        temporal = temporal + jnp.einsum(
            "fhwc,cd->fhwd",
            picked,
            time_full[:, tap * chans : (tap + 1) * chans],
            preferred_element_type=jnp.float32,
        )
    resid = (video.astype(jnp.float32) + temporal).astype(jnp.bfloat16)
    mean_two, scale_two = group_moments(resid)
    pixels = height * width
    flat_resid = resid.reshape(frames, pixels, chans)
    resid_time = lax.all_to_all(flat_resid, "tm", split_axis=1, concat_axis=0, tiled=True)
    moments = lax.all_gather(jnp.stack([mean_two, scale_two]), "tm", axis=1, tiled=True)
    wide = jnp.repeat(moments, chans // GROUPS, axis=2)
    flat_norm = (
        (resid_time.astype(jnp.float32) - wide[0][:, None]) * wide[1][:, None] * norm_gains[1]
    ).astype(jnp.bfloat16)
    qkv_time = jnp.einsum(
        "fpc,cd->fpd", flat_norm, qkv_full, preferred_element_type=jnp.float32
    ).astype(jnp.bfloat16)
    query = qkv_time[..., :chans]
    keys = qkv_time[..., chans : 2 * chans]
    value_rows = qkv_time[..., 2 * chans :]
    index = jnp.arange(total_frames, dtype=jnp.int32)
    allowed = (index[None, :] <= index[:, None]) & (index[None, :] >= starts[:, None])
    scores = jnp.einsum(
        "fpc,gpc->pfg", query, keys, preferred_element_type=jnp.float32
    ) / math.sqrt(chans)
    scores = jnp.where(allowed[None], scores, -1e30)
    top = jnp.max(scores, axis=-1, keepdims=True)
    expo = jnp.where(allowed[None], jnp.exp(scores - top), 0.0)
    attention_probabilities = (expo / jnp.sum(expo, axis=-1, keepdims=True)).astype(jnp.bfloat16)
    attention_output = jnp.einsum(
        "boh,hba->boa", attention_probabilities, value_rows, preferred_element_type=jnp.float32
    ).astype(jnp.bfloat16)
    projected_output = jnp.einsum(
        "axi,iy->axy", attention_output, output_complete, preferred_element_type=jnp.float32
    )
    mixed = (jnp.swapaxes(resid_time, 0, 1).astype(jnp.float32) + projected_output).astype(
        jnp.bfloat16
    )
    return mixed.reshape(1, 1, mixed.shape[0], total_frames, chans)


def solution(mesh):
    return jax.shard_map(
        body,
        mesh=mesh,
        in_specs=(
            P("tm", "band", "fsdp", None),
            P(),
            P(),
            P(("band", "fsdp"), None),
            P(("band", "fsdp"), None),
            P(("band", "fsdp"), None),
            P(("band", "fsdp"), None),
        ),
        out_specs=P("band", "fsdp", "tm", None, None),
        check_vma=False,
    )
```

```python
import math

import jax
import jax.numpy as jnp
from jax import lax
from jax.experimental import pallas as pl
from jax.experimental.pallas import tpu as pltpu
from jax.sharding import PartitionSpec as P

GROUPS = 32


EPS = 1e-06


def with_halo(x, sides, width):
    for axis, dim in sides:
        size, length = (lax.axis_size(axis), x.shape[dim])
        up = [(i, (i + 1) % size) for i in range(size - 1)]
        down = [(j, i) for i, j in up]
        last = lax.slice_in_dim(x, length - width, length, axis=dim)
        initial = lax.slice_in_dim(x, 0, width, axis=dim)
        before = lax.ppermute(last, axis, up)
        after = lax.ppermute(initial, axis, down)
        x = jnp.concatenate([before, x, after], axis=dim)
    return x


def from_behind(x, axis, by):
    length = lax.axis_size(axis)
    pairs = [(i, i + by) for i in range(length) if 0 <= i + by < length]
    return lax.ppermute(x, axis, pairs)


def frame_starts(clip_lengths, total):
    ends = jnp.cumsum(clip_lengths)
    begins = ends - clip_lengths
    index = jnp.arange(total, dtype=jnp.int32)
    chosen = jnp.where(begins[None, :] <= index[:, None], begins[None, :], 0)
    return jnp.max(chosen, axis=1)


def group_moments(field):
    frames, height, width, chans = field.shape
    group_width = chans // GROUPS
    vals = field.astype(jnp.float32).reshape(frames, height * width, GROUPS, group_width)
    sums = jnp.sum(vals, axis=(1, 3))
    squares = jnp.sum(vals * vals, axis=(1, 3))
    sums, squares = lax.psum((sums, squares), ("band", "fsdp"))
    count = height * width * group_width * lax.axis_size("band") * lax.axis_size("fsdp")
    mean = sums / count
    scale = lax.rsqrt(squares / count - mean * mean + EPS)
    return (mean, scale)


def apply_norm(field, mean, scale, gain):
    shape = field.shape
    chans = shape[-1]
    group_width = chans // GROUPS
    vals = field.astype(jnp.float32).reshape(shape[0], -1, GROUPS, group_width)
    normed = (vals - mean[:, None, :, None]) * scale[:, None, :, None]
    return normed.reshape(shape) * gain


def body(video, clip_lengths, norm_gains, spatial_kernel_weight, w_time, w_qkv, w_out):
    space_full, time_full, qkv_full, output_complete = (
        lax.all_gather(spatial_kernel_weight, ("band", "fsdp"), axis=0, tiled=True),
        lax.all_gather(w_time, ("band", "fsdp"), axis=0, tiled=True),
        lax.all_gather(w_qkv, ("band", "fsdp"), axis=0, tiled=True),
        lax.all_gather(w_out, ("band", "fsdp"), axis=0, tiled=True),
    )
    frames, height, width, chans = video.shape
    ranks = lax.axis_size("tm")
    total_frames = frames * ranks
    first = lax.axis_index("tm") * frames
    starts = frame_starts(clip_lengths, total_frames)
    local_starts = lax.dynamic_slice_in_dim(starts, first, frames)
    mean_one, scale_one = group_moments(video)
    act = jax.nn.silu(apply_norm(video, mean_one, scale_one, norm_gains[0])).astype(jnp.bfloat16)
    padded = with_halo(act, (("band", 1), ("fsdp", 2)), 1)
    spatial = jnp.zeros((frames, height, width, chans), jnp.float32)
    for tap in range(9):
        shift_y = tap // 3
        shift_x = tap % 3
        spatial = spatial + jnp.einsum(
            "fhwc,cd->fhwd",
            padded[:, shift_y : shift_y + height, shift_x : shift_x + width],
            space_full[:, tap * chans : (tap + 1) * chans],
            preferred_element_type=jnp.float32,
        )
    spatial = spatial.astype(jnp.bfloat16)
    carried = from_behind(spatial[frames - 2 :], "tm", 1)
    extended = jnp.concatenate([carried, spatial], axis=0)
    position = first + jnp.arange(frames, dtype=jnp.int32)
    slots = jnp.arange(frames + 2, dtype=jnp.int32)
    temporal = jnp.zeros((frames, height, width, chans), jnp.float32)
    for tap in range(3):
        source = jnp.maximum(position - 2 + tap, local_starts) - first + 2
        select = (source[:, None] == slots[None, :]).astype(jnp.bfloat16)
        picked = jnp.einsum(
            "fe,ehwc->fhwc", select, extended, preferred_element_type=jnp.float32
        ).astype(jnp.bfloat16)
        temporal = temporal + jnp.einsum(
            "fhwc,cd->fhwd",
            picked,
            time_full[:, tap * chans : (tap + 1) * chans],
            preferred_element_type=jnp.float32,
        )
    resid = (video.astype(jnp.float32) + temporal).astype(jnp.bfloat16)
    mean_two, scale_two = group_moments(resid)
    pixels = height * width
    flat_resid = resid.reshape(frames, pixels, chans)
    resid_time = lax.all_to_all(flat_resid, "tm", split_axis=1, concat_axis=0, tiled=True)
    moments = lax.all_gather(jnp.stack([mean_two, scale_two]), "tm", axis=1, tiled=True)
    wide = jnp.repeat(moments, chans // GROUPS, axis=2)
    flat_norm = (
        (resid_time.astype(jnp.float32) - wide[0][:, None]) * wide[1][:, None] * norm_gains[1]
    ).astype(jnp.bfloat16)
    qkv_time = jnp.einsum(
        "fpc,cd->fpd", flat_norm, qkv_full, preferred_element_type=jnp.float32
    ).astype(jnp.bfloat16)
    query = qkv_time[..., :chans]
    keys = qkv_time[..., chans : 2 * chans]
    value_rows = qkv_time[..., 2 * chans :]
    index = jnp.arange(total_frames, dtype=jnp.int32)
    allowed = (index[None, :] <= index[:, None]) & (index[None, :] >= starts[:, None])
    scores = jnp.einsum(
        "fpc,gpc->pfg", query, keys, preferred_element_type=jnp.float32
    ) / math.sqrt(chans)
    scores = jnp.where(allowed[None], scores, -1e30)
    top = jnp.max(scores, axis=-1, keepdims=True)
    expo = jnp.where(allowed[None], jnp.exp(scores - top), 0.0)
    attention_probabilities = (expo / jnp.sum(expo, axis=-1, keepdims=True)).astype(jnp.bfloat16)
    attention_output = jnp.einsum(
        "boh,hba->boa", attention_probabilities, value_rows, preferred_element_type=jnp.float32
    ).astype(jnp.bfloat16)
    projected_output = jnp.einsum(
        "axi,iy->axy", attention_output, output_complete, preferred_element_type=jnp.float32
    )
    mixed = (jnp.swapaxes(resid_time, 0, 1).astype(jnp.float32) + projected_output).astype(
        jnp.bfloat16
    )
    return mixed.reshape(1, 1, mixed.shape[0], total_frames, chans)

HIGH = lax.Precision.HIGHEST
VMEM_BYTES = 56 * 1024 * 1024


def scalar_starts(lengths, first, count):
    begins, at = [], jnp.int32(0)
    for clip in range(lengths.shape[0]):
        begins.append(at)
        at = at + lengths[clip]
    out = []
    for i in range(count):
        start = jnp.int32(0)
        for begin in begins:
            start = jnp.where(begin <= first + i, jnp.maximum(start, begin), start)
        out.append(start)
    return out


def spread(rows, cols, of_row, of_col):
    r = of_row(lax.broadcasted_iota(jnp.int32, (rows, cols), 0))
    c = of_col(lax.broadcasted_iota(jnp.int32, (rows, cols), 1))
    return jnp.where(r == c, 1.0, 0.0).astype(jnp.float32)


def sum_rows(x):
    return jnp.sum(x.reshape(x.shape[0] // 8, 8, x.shape[1]), axis=0)


def front_kernel(n, lengths, video, gains, w_space, w_time, got, got_sums,
                 act, ext, res, sums, ws, wt, w_sem, halo_sem, send_sem, recv_sem):
    frames, height, width, chans = video.shape
    pixels = height * width
    per = pixels // n
    half = frames // 2
    gw = chans // GROUPS
    me = lax.axis_index("tm")
    barrier = pltpu.get_barrier_semaphore()

    def greet(j, c):
        pl.semaphore_signal(barrier, inc=1, device_id={"tm": lax.rem(me + j, n)},
                            device_id_type=pl.DeviceIdType.MESH)
        return c

    lax.fori_loop(1, n, greet, 0)
    loads = []
    for tap in range(9):
        loads.append(pltpu.make_async_copy(
            w_space.at[:, pl.ds(tap * chans, chans)], ws.at[pl.ds(tap * chans, chans)], w_sem.at[tap]))
    for tap in range(3):
        loads.append(pltpu.make_async_copy(
            w_time.at[:, pl.ds(tap * chans, chans)], wt.at[pl.ds(tap * chans, chans)], w_sem.at[9 + tap]))
    for load in loads:
        load.start()

    group = spread(chans, chans, lambda r: r // gw, lambda c: c // gw)
    rows = 4
    step = rows * width
    column = lax.rem(lax.broadcasted_iota(jnp.int32, (step, chans), 0), width)
    gain = gains[0:1, :]
    zero_row = jnp.zeros((1, width, 3 * chans), jnp.bfloat16)

    def norm_act(f):
        def moment(i, acc):
            v = video[f, pl.ds(i * rows, rows)].reshape(step, chans).astype(jnp.float32)
            return acc[0] + sum_rows(v), acc[1] + sum_rows(v * v)

        zero = jnp.zeros((8, chans), jnp.float32)
        total, square = lax.fori_loop(0, height // rows, moment, (zero, zero), unroll=True)
        both = jnp.concatenate([total, square], axis=0)
        both = lax.dot(both, group, precision=HIGH, preferred_element_type=jnp.float32)
        count = pixels * gw
        mean = jnp.sum(both[:8], axis=0, keepdims=True) / count
        second = jnp.sum(both[8:], axis=0, keepdims=True) / count
        scale = lax.rsqrt(second - mean * mean + EPS) * gain
        act[f, 0:1] = zero_row
        act[f, height + 1:height + 2] = zero_row

        def put(i, c):
            v = video[f, pl.ds(i * rows, rows)].reshape(step, chans).astype(jnp.float32)
            v = (v - mean) * scale
            v = v * (0.5 + 0.5 * jnp.tanh(0.5 * v))
            left = jnp.where(column == 0, 0.0, pltpu.roll(v, 1, 0))
            right = jnp.where(column == width - 1, 0.0, pltpu.roll(v, step - 1, 0))
            for side, value in enumerate((left, v, right)):
                act[f, pl.ds(1 + i * rows, rows), :, side * chans:(side + 1) * chans] = (
                    value.astype(jnp.bfloat16).reshape(rows, width, chans))
            return c

        lax.fori_loop(0, height // rows, put, 0, unroll=True)

    def conv(f):
        total = None
        for dy in range(3):
            part = jnp.dot(act[f, dy:dy + height].reshape(pixels, 3 * chans),
                           ws[dy * 3 * chans:(dy + 1) * 3 * chans],
                           preferred_element_type=jnp.float32)
            total = part if total is None else total + part
        ext[2 + f] = total.astype(jnp.bfloat16)

    halo = pltpu.make_async_remote_copy(
        src_ref=ext.at[pl.ds(frames, 2)], dst_ref=ext.at[pl.ds(0, 2)],
        send_sem=halo_sem.at[0], recv_sem=halo_sem.at[1],
        device_id={"tm": lax.rem(me + 1, n)}, device_id_type=pl.DeviceIdType.MESH)

    norm_act(2)
    norm_act(3)
    for load in loads:
        load.wait()
    conv(2)
    conv(3)
    pl.semaphore_wait(barrier, n - 1)

    @pl.when(me < n - 1)
    def _():
        halo.start()

    norm_act(0)
    norm_act(1)
    conv(0)
    conv(1)

    first = me * frames
    starts = scalar_starts(lengths, first, frames)

    def residual(f):
        own, one, two = ext[2 + f], ext[1 + f], ext[f]
        near = jnp.where(starts[f] <= first + f - 1, one, own)
        far = jnp.where(starts[f] <= first + f - 2, two, near)
        temporal = jnp.dot(jnp.concatenate([far, near, own], axis=1), wt[...],
                           preferred_element_type=jnp.float32)
        r = video[f].reshape(pixels, chans).astype(jnp.float32) + temporal
        r = r.astype(jnp.bfloat16)
        res[f // half, :, f % half] = r.reshape(n, per, chans)
        r = r.astype(jnp.float32)
        return sum_rows(r), sum_rows(r * r)

    def send(part):
        def one(j, c):
            d = lax.rem(me + j, n)
            pltpu.make_async_remote_copy(
                src_ref=res.at[part, d], dst_ref=got.at[part, me],
                send_sem=send_sem.at[part], recv_sem=recv_sem.at[part],
                device_id={"tm": d}, device_id_type=pl.DeviceIdType.MESH).start()
            return c

        lax.fori_loop(1, n, one, 0)
        pltpu.make_async_copy(res.at[part, me], got.at[part, me], recv_sem.at[part]).start()

    stat = {}
    stat[2] = residual(2)
    stat[3] = residual(3)
    send(1)

    @pl.when(me > 0)
    def _():
        halo.wait_recv()

    stat[0] = residual(0)
    stat[1] = residual(1)
    send(0)

    low = spread(chans, 128, lambda r: r // gw, lambda c: c)
    high = spread(chans, 128, lambda r: r // gw + GROUPS, lambda c: c)
    total = jnp.concatenate([jnp.sum(stat[f][0], axis=0, keepdims=True) for f in range(frames)]
                            + [jnp.zeros((8 - frames, chans), jnp.float32)], axis=0)
    square = jnp.concatenate([jnp.sum(stat[f][1], axis=0, keepdims=True) for f in range(frames)]
                             + [jnp.zeros((8 - frames, chans), jnp.float32)], axis=0)
    sums[...] = (lax.dot(total, low, precision=HIGH, preferred_element_type=jnp.float32)
                 + lax.dot(square, high, precision=HIGH, preferred_element_type=jnp.float32))

    def tell(j, c):
        pltpu.make_async_remote_copy(
            src_ref=sums, dst_ref=got_sums.at[me], send_sem=send_sem.at[2], recv_sem=recv_sem.at[2],
            device_id={"tm": lax.rem(me + j, n)}, device_id_type=pl.DeviceIdType.MESH).start()
        return c

    lax.fori_loop(1, n, tell, 0)
    pltpu.make_async_copy(sums, got_sums.at[me], recv_sem.at[2]).start()

    @pl.when(me < n - 1)
    def _():
        halo.wait_send()

    for part in range(2):
        pltpu.make_async_copy(got.at[part, pl.ds(0, n - 1)], got.at[part, pl.ds(0, n - 1)],
                              send_sem.at[part]).wait()
        pltpu.make_async_copy(got.at[part], got.at[part], recv_sem.at[part]).wait()
    pltpu.make_async_copy(got_sums.at[pl.ds(0, n - 1)], got_sums.at[pl.ds(0, n - 1)],
                          send_sem.at[2]).wait()
    pltpu.make_async_copy(got_sums, got_sums, recv_sem.at[2]).wait()


def front(n, lengths, video, gains, w_space, w_time):
    frames, height, width, chans = video.shape
    pixels = height * width
    per = pixels // n
    half = frames // 2
    vmem = pl.BlockSpec(memory_space=pltpu.VMEM)
    anyw = pl.BlockSpec(memory_space=pl.ANY)
    bf16 = jnp.bfloat16
    return pl.pallas_call(
        lambda *refs: front_kernel(n, *refs),
        out_shape=(jax.ShapeDtypeStruct((2, n, half, per, chans), bf16),
                   jax.ShapeDtypeStruct((n, 8, 128), jnp.float32)),
        in_specs=[pl.BlockSpec(memory_space=pltpu.SMEM), vmem, vmem, anyw, anyw],
        out_specs=(anyw, anyw),
        scratch_shapes=[
            pltpu.VMEM((frames, height + 2, width, 3 * chans), bf16),
            pltpu.VMEM((frames + 2, pixels, chans), bf16),
            pltpu.VMEM((2, n, half, per, chans), bf16),
            pltpu.VMEM((8, 128), jnp.float32),
            pltpu.VMEM((9 * chans, chans), bf16),
            pltpu.VMEM((3 * chans, chans), bf16),
            pltpu.SemaphoreType.DMA((12,)),
            pltpu.SemaphoreType.DMA((2,)),
            pltpu.SemaphoreType.DMA((3,)),
            pltpu.SemaphoreType.DMA((3,)),
        ],
        compiler_params=pltpu.CompilerParams(
            collective_id=0, has_side_effects=True, vmem_limit_bytes=VMEM_BYTES),
        cost_estimate=pl.CostEstimate(flops=3_300_000_000, bytes_accessed=4_000_000, transcendentals=600_000),
        name="front",
    )(lengths, video, gains, w_space, w_time)


def tail_kernel(lengths, got, got_sums, gains, w_qkv, w_out, out, flat, mean, scale, open_):
    _, n, half, per, chans = got.shape
    frames = 2 * half
    total = n * frames
    gw = chans // GROUPS
    count = out.shape[2]

    @pl.when(pl.program_id(0) == 0)
    def _():
        block = 16
        srcs = block // frames
        side = block * per

        def frame_of(r):
            part, rest = r // (srcs * half * per), lax.rem(r, srcs * half * per)
            src, rest = rest // (half * per), lax.rem(rest, half * per)
            return src * frames + part * half + rest // per, lax.rem(rest, per)

        def place(c):
            f, p = frame_of(c)
            return p * block + f

        perm = spread(side, side, lambda r: r, place).astype(jnp.bfloat16)
        for b in range(total // block):
            x = jnp.concatenate(
                [got[h, b * srcs:(b + 1) * srcs].reshape(srcs * half * per, chans) for h in range(2)], axis=0)
            y = jnp.dot(perm, x, preferred_element_type=jnp.float32).astype(jnp.bfloat16)
            flat[:, b * block:(b + 1) * block, :] = y.reshape(per, block, chans)
        m = None
        stats = got_sums[...].reshape(n * 8, 128)
        pick = spread(total, n * 8, lambda r: r // frames * 8 + lax.rem(r, frames), lambda c: c)
        stats = lax.dot(pick, stats, precision=HIGH, preferred_element_type=jnp.float32)
        low = spread(128, chans, lambda r: r, lambda c: c // gw)
        high = spread(128, chans, lambda r: r, lambda c: c // gw + GROUPS)
        number = total_pixels(n, per) * gw
        mu = lax.dot(stats, low, precision=HIGH, preferred_element_type=jnp.float32) / number
        sq = lax.dot(stats, high, precision=HIGH, preferred_element_type=jnp.float32) / number
        mean[...] = mu
        scale[...] = lax.rsqrt(sq - mu * mu + EPS) * gains[1:2, :]
        f = lax.broadcasted_iota(jnp.int32, (total, total), 0)
        g = lax.broadcasted_iota(jnp.int32, (total, total), 1)
        start = jnp.zeros((total, total), jnp.int32)
        at = jnp.int32(0)
        for clip in range(lengths.shape[0]):
            start = jnp.where(at <= f, at, start)
            at = at + lengths[clip]
        open_[...] = jnp.where((g <= f) & (g >= start), 0.0, -1e30)

    base = pl.program_id(0) * count
    x = flat[pl.ds(base, count)]
    normed = ((x.astype(jnp.float32) - mean[...][None]) * scale[...][None]).astype(jnp.bfloat16)
    qkv = jnp.dot(normed.reshape(count * total, chans), w_qkv[...], preferred_element_type=jnp.float32)
    query = (qkv[:, :chans] * (1.0 / math.sqrt(chans))).astype(jnp.bfloat16).reshape(count, total, chans)
    keys = qkv[:, chans:2 * chans].astype(jnp.bfloat16).reshape(count, total, chans)
    values = qkv[:, 2 * chans:].astype(jnp.bfloat16).reshape(count, total, chans)
    shut = open_[...]
    attn = []
    for p in range(count):
        score = lax.dot_general(query[p], keys[p], (((1,), (1,)), ((), ())),
                                preferred_element_type=jnp.float32)
        score = jnp.where(shut == 0.0, score, -1e30)
        top = jnp.max(score, axis=1, keepdims=True)
        expo = jnp.exp(score - top)
        prob = (expo * (1.0 / jnp.sum(expo, axis=1, keepdims=True))).astype(jnp.bfloat16)
        attn.append(jnp.dot(prob, values[p], preferred_element_type=jnp.float32).astype(jnp.bfloat16))
    attn = jnp.concatenate(attn, axis=0)
    proj = jnp.dot(attn, w_out[...], preferred_element_type=jnp.float32)
    mixed = x.astype(jnp.float32) + proj.reshape(count, total, chans)
    out[...] = mixed.astype(jnp.bfloat16).reshape(out.shape)


def total_pixels(n, per):
    return n * per


def tail(lengths, got, got_sums, gains, w_qkv, w_out):
    _, n, half, per, chans = got.shape
    total = n * 2 * half
    count = 4 if per % 4 == 0 else 1
    vmem = pl.BlockSpec(memory_space=pltpu.VMEM)
    return pl.pallas_call(
        tail_kernel,
        grid=(per // count,),
        out_shape=jax.ShapeDtypeStruct((1, 1, per, total, chans), jnp.bfloat16),
        in_specs=[pl.BlockSpec(memory_space=pltpu.SMEM), vmem, vmem, vmem, vmem, vmem],
        out_specs=pl.BlockSpec((1, 1, count, total, chans), lambda i: (0, 0, i, 0, 0)),
        scratch_shapes=[
            pltpu.VMEM((per, total, chans), jnp.bfloat16),
            pltpu.VMEM((total, chans), jnp.float32),
            pltpu.VMEM((total, chans), jnp.float32),
            pltpu.VMEM((total, total), jnp.float32),
        ],
        compiler_params=pltpu.CompilerParams(vmem_limit_bytes=VMEM_BYTES),
        name="tail",
    )(lengths, got, got_sums, gains, w_qkv, w_out)


def whole_image(video, clip_lengths, norm_gains, spatial_kernel_weight, w_time, w_qkv, w_out):
    n = lax.axis_size("tm")
    got, got_sums = front(n, clip_lengths, video, norm_gains, spatial_kernel_weight, w_time)
    return tail(clip_lengths, got, got_sums, norm_gains, w_qkv, w_out)


def solution(mesh):
    alone = mesh.shape["band"] * mesh.shape["fsdp"] == 1
    return jax.shard_map(
        whole_image if alone else body,
        mesh=mesh,
        in_specs=(
            P("tm", "band", "fsdp", None),
            P(),
            P(),
            P(("band", "fsdp"), None),
            P(("band", "fsdp"), None),
            P(("band", "fsdp"), None),
            P(("band", "fsdp"), None),
        ),
        out_specs=P("band", "fsdp", "tm", None, None),
        check_vma=False,
    )
```

```python
import math

import jax
import jax.numpy as jnp
from jax import lax
from jax.experimental import pallas as pl
from jax.experimental.pallas import tpu as pltpu
from jax.sharding import PartitionSpec as P

GROUPS = 32


EPS = 1e-06


def with_halo(x, sides, width):
    for axis, dim in sides:
        size, length = (lax.axis_size(axis), x.shape[dim])
        up = [(i, (i + 1) % size) for i in range(size - 1)]
        down = [(j, i) for i, j in up]
        last = lax.slice_in_dim(x, length - width, length, axis=dim)
        initial = lax.slice_in_dim(x, 0, width, axis=dim)
        before = lax.ppermute(last, axis, up)
        after = lax.ppermute(initial, axis, down)
        x = jnp.concatenate([before, x, after], axis=dim)
    return x


def from_behind(x, axis, by):
    length = lax.axis_size(axis)
    pairs = [(i, i + by) for i in range(length) if 0 <= i + by < length]
    return lax.ppermute(x, axis, pairs)


def frame_starts(clip_lengths, total):
    ends = jnp.cumsum(clip_lengths)
    begins = ends - clip_lengths
    index = jnp.arange(total, dtype=jnp.int32)
    chosen = jnp.where(begins[None, :] <= index[:, None], begins[None, :], 0)
    return jnp.max(chosen, axis=1)


def group_moments(field):
    frames, height, width, chans = field.shape
    group_width = chans // GROUPS
    vals = field.astype(jnp.float32).reshape(frames, height * width, GROUPS, group_width)
    sums = jnp.sum(vals, axis=(1, 3))
    squares = jnp.sum(vals * vals, axis=(1, 3))
    sums, squares = lax.psum((sums, squares), ("band", "fsdp"))
    count = height * width * group_width * lax.axis_size("band") * lax.axis_size("fsdp")
    mean = sums / count
    scale = lax.rsqrt(squares / count - mean * mean + EPS)
    return (mean, scale)


def apply_norm(field, mean, scale, gain):
    shape = field.shape
    chans = shape[-1]
    group_width = chans // GROUPS
    vals = field.astype(jnp.float32).reshape(shape[0], -1, GROUPS, group_width)
    normed = (vals - mean[:, None, :, None]) * scale[:, None, :, None]
    return normed.reshape(shape) * gain


def body(video, clip_lengths, norm_gains, spatial_kernel_weight, w_time, w_qkv, w_out):
    space_full, time_full, qkv_full, output_complete = (
        lax.all_gather(spatial_kernel_weight, ("band", "fsdp"), axis=0, tiled=True),
        lax.all_gather(w_time, ("band", "fsdp"), axis=0, tiled=True),
        lax.all_gather(w_qkv, ("band", "fsdp"), axis=0, tiled=True),
        lax.all_gather(w_out, ("band", "fsdp"), axis=0, tiled=True),
    )
    frames, height, width, chans = video.shape
    ranks = lax.axis_size("tm")
    total_frames = frames * ranks
    first = lax.axis_index("tm") * frames
    starts = frame_starts(clip_lengths, total_frames)
    local_starts = lax.dynamic_slice_in_dim(starts, first, frames)
    mean_one, scale_one = group_moments(video)
    act = jax.nn.silu(apply_norm(video, mean_one, scale_one, norm_gains[0])).astype(jnp.bfloat16)
    padded = with_halo(act, (("band", 1), ("fsdp", 2)), 1)
    spatial = jnp.zeros((frames, height, width, chans), jnp.float32)
    for tap in range(9):
        shift_y = tap // 3
        shift_x = tap % 3
        spatial = spatial + jnp.einsum(
            "fhwc,cd->fhwd",
            padded[:, shift_y : shift_y + height, shift_x : shift_x + width],
            space_full[:, tap * chans : (tap + 1) * chans],
            preferred_element_type=jnp.float32,
        )
    spatial = spatial.astype(jnp.bfloat16)
    carried = from_behind(spatial[frames - 2 :], "tm", 1)
    extended = jnp.concatenate([carried, spatial], axis=0)
    position = first + jnp.arange(frames, dtype=jnp.int32)
    slots = jnp.arange(frames + 2, dtype=jnp.int32)
    temporal = jnp.zeros((frames, height, width, chans), jnp.float32)
    for tap in range(3):
        source = jnp.maximum(position - 2 + tap, local_starts) - first + 2
        select = (source[:, None] == slots[None, :]).astype(jnp.bfloat16)
        picked = jnp.einsum(
            "fe,ehwc->fhwc", select, extended, preferred_element_type=jnp.float32
        ).astype(jnp.bfloat16)
        temporal = temporal + jnp.einsum(
            "fhwc,cd->fhwd",
            picked,
            time_full[:, tap * chans : (tap + 1) * chans],
            preferred_element_type=jnp.float32,
        )
    resid = (video.astype(jnp.float32) + temporal).astype(jnp.bfloat16)
    mean_two, scale_two = group_moments(resid)
    pixels = height * width
    flat_resid = resid.reshape(frames, pixels, chans)
    resid_time = lax.all_to_all(flat_resid, "tm", split_axis=1, concat_axis=0, tiled=True)
    moments = lax.all_gather(jnp.stack([mean_two, scale_two]), "tm", axis=1, tiled=True)
    wide = jnp.repeat(moments, chans // GROUPS, axis=2)
    flat_norm = (
        (resid_time.astype(jnp.float32) - wide[0][:, None]) * wide[1][:, None] * norm_gains[1]
    ).astype(jnp.bfloat16)
    qkv_time = jnp.einsum(
        "fpc,cd->fpd", flat_norm, qkv_full, preferred_element_type=jnp.float32
    ).astype(jnp.bfloat16)
    query = qkv_time[..., :chans]
    keys = qkv_time[..., chans : 2 * chans]
    value_rows = qkv_time[..., 2 * chans :]
    index = jnp.arange(total_frames, dtype=jnp.int32)
    allowed = (index[None, :] <= index[:, None]) & (index[None, :] >= starts[:, None])
    scores = jnp.einsum(
        "fpc,gpc->pfg", query, keys, preferred_element_type=jnp.float32
    ) / math.sqrt(chans)
    scores = jnp.where(allowed[None], scores, -1e30)
    top = jnp.max(scores, axis=-1, keepdims=True)
    expo = jnp.where(allowed[None], jnp.exp(scores - top), 0.0)
    attention_probabilities = (expo / jnp.sum(expo, axis=-1, keepdims=True)).astype(jnp.bfloat16)
    attention_output = jnp.einsum(
        "boh,hba->boa", attention_probabilities, value_rows, preferred_element_type=jnp.float32
    ).astype(jnp.bfloat16)
    projected_output = jnp.einsum(
        "axi,iy->axy", attention_output, output_complete, preferred_element_type=jnp.float32
    )
    mixed = (jnp.swapaxes(resid_time, 0, 1).astype(jnp.float32) + projected_output).astype(
        jnp.bfloat16
    )
    return mixed.reshape(1, 1, mixed.shape[0], total_frames, chans)

HIGH = lax.Precision.HIGHEST
VMEM_BYTES = 56 * 1024 * 1024


def scalar_starts(lengths, first, count):
    begins, at = [], jnp.int32(0)
    for clip in range(lengths.shape[0]):
        begins.append(at)
        at = at + lengths[clip]
    out = []
    for i in range(count):
        start = jnp.int32(0)
        for begin in begins:
            start = jnp.where(begin <= first + i, jnp.maximum(start, begin), start)
        out.append(start)
    return out


def over(x, k):
    return x >> (k.bit_length() - 1) if k & (k - 1) == 0 else x // k


def left_of(x, k):
    return x & (k - 1) if k & (k - 1) == 0 else lax.rem(x, k)


def spread(rows, cols, of_row, of_col):
    r = of_row(lax.broadcasted_iota(jnp.int32, (rows, cols), 0))
    c = of_col(lax.broadcasted_iota(jnp.int32, (rows, cols), 1))
    return jnp.where(r == c, 1.0, 0.0).astype(jnp.float32)


def exact_dot(a, b):
    return lax.dot(a, b, precision=HIGH, preferred_element_type=jnp.float32)


def sum_rows(x):
    return jnp.sum(x.reshape(x.shape[0] // 8, 8, x.shape[1]), axis=0)


def kernel(n, lengths, video, gains, w_space, w_time, w_qkv, w_out, out,
           before, act, ext, res_a, res_b, got_a, got_b, sums, got_sums, ws, wt, flat, done,
           mean_all, scale_all, shut, w_sem, halo_sem, send_sem, recv_sem, out_sem):
    frames, height, width, chans = video.shape
    pixels = height * width
    per = pixels // n
    part_px = per // 2
    gw = chans // GROUPS
    total = n * frames
    me = lax.axis_index("tm")
    barrier = pltpu.get_barrier_semaphore()

    def greet(j, c):
        pl.semaphore_signal(barrier, inc=1, device_id={"tm": lax.rem(me + j, n)},
                            device_id_type=pl.DeviceIdType.MESH)
        return c

    lax.fori_loop(1, n, greet, 0)
    loads = []
    for tap in range(9):
        loads.append(pltpu.make_async_copy(
            w_space.at[:, pl.ds(tap * chans, chans)], ws.at[pl.ds(tap * chans, chans)], w_sem.at[tap]))
    for tap in range(3):
        loads.append(pltpu.make_async_copy(
            w_time.at[:, pl.ds(tap * chans, chans)], wt.at[pl.ds(tap * chans, chans)], w_sem.at[9 + tap]))
    for load in loads:
        load.start()

    group = spread(chans, chans, lambda r: over(r, gw), lambda c: over(c, gw))
    rows = 4
    step = rows * width
    column = left_of(lax.broadcasted_iota(jnp.int32, (step, chans), 0), width)
    gain = gains[0:1, :]
    zero_row = jnp.zeros((1, width, 3 * chans), jnp.bfloat16)

    def norm_act(source, f, slot):
        def moment(i, acc):
            v = source[f, pl.ds(i * rows, rows)].reshape(step, chans).astype(jnp.float32)
            return acc[0] + sum_rows(v), acc[1] + sum_rows(v * v)

        zero = jnp.zeros((8, chans), jnp.float32)
        one, two = lax.fori_loop(0, height // rows, moment, (zero, zero), unroll=True)
        both = exact_dot(jnp.concatenate([one, two], axis=0), group)
        count = pixels * gw
        mean = jnp.sum(both[:8], axis=0, keepdims=True) / count
        second = jnp.sum(both[8:], axis=0, keepdims=True) / count
        scale = lax.rsqrt(second - mean * mean + EPS) * gain
        act[slot, 0:1] = zero_row
        act[slot, height + 1:height + 2] = zero_row

        def put(i, c):
            v = source[f, pl.ds(i * rows, rows)].reshape(step, chans).astype(jnp.float32)
            v = (v - mean) * scale
            v = v * (0.5 + 0.5 * jnp.tanh(0.5 * v))
            left = jnp.where(column == 0, 0.0, pltpu.roll(v, 1, 0))
            right = jnp.where(column == width - 1, 0.0, pltpu.roll(v, step - 1, 0))
            for side, value in enumerate((left, v, right)):
                act[slot, pl.ds(1 + i * rows, rows), :, side * chans:(side + 1) * chans] = (
                    value.astype(jnp.bfloat16).reshape(rows, width, chans))
            return c

        lax.fori_loop(0, height // rows, put, 0, unroll=True)

    def conv(slot, to):
        acc = None
        for dy in range(3):
            part = jnp.dot(act[slot, dy:dy + height].reshape(pixels, 3 * chans),
                           ws[dy * 3 * chans:(dy + 1) * 3 * chans],
                           preferred_element_type=jnp.float32)
            acc = part if acc is None else acc + part
        ext[to] = acc.astype(jnp.bfloat16)

    halo = pltpu.make_async_remote_copy(
        src_ref=video.at[pl.ds(frames - 2, 2)], dst_ref=before,
        send_sem=halo_sem.at[0], recv_sem=halo_sem.at[1],
        device_id={"tm": lax.rem(me + 1, n)}, device_id_type=pl.DeviceIdType.MESH)

    norm_act(video, 0, 0)
    pl.semaphore_wait(barrier, n - 1)

    @pl.when(me < n - 1)
    def _():
        halo.start()

    for f in range(1, frames):
        norm_act(video, f, f)
    for load in loads:
        load.wait()
    for f in range(frames):
        conv(f, 2 + f)

    first = me * frames
    starts = scalar_starts(lengths, first, frames)
    stat = {}

    def residual(f):
        own, one, two = ext[2 + f], ext[1 + f], ext[f]
        near = jnp.where(starts[f] <= first + f - 1, one, own)
        far = jnp.where(starts[f] <= first + f - 2, two, near)
        temporal = jnp.dot(jnp.concatenate([far, near, own], axis=1), wt[...],
                           preferred_element_type=jnp.float32)
        r = video[f].reshape(pixels, chans).astype(jnp.float32) + temporal
        r = r.astype(jnp.bfloat16).astype(jnp.float32)
        stat[f] = jnp.concatenate([sum_rows(r), sum_rows(r * r)], axis=0)
        return r.reshape(n, 2, part_px, chans)

    def pair(part):
        r = [residual(2 * part + i) for i in range(2)]
        res_a[part] = jnp.concatenate([r[0][:, 0], r[1][:, 0]], axis=1).astype(jnp.bfloat16)
        res_b[:, 2 * part * part_px:2 * (part + 1) * part_px] = (
            jnp.concatenate([r[0][:, 1], r[1][:, 1]], axis=1).astype(jnp.bfloat16))

    def exchange(source, target, which, picked):
        def one(j, c):
            d = lax.rem(me + j, n)
            pltpu.make_async_remote_copy(
                src_ref=source.at[d] if picked else source, dst_ref=target.at[me],
                send_sem=send_sem.at[which], recv_sem=recv_sem.at[which],
                device_id={"tm": d}, device_id_type=pl.DeviceIdType.MESH).start()
            return c

        lax.fori_loop(1, n, one, 0)
        pltpu.make_async_copy(source.at[me] if picked else source, target.at[me],
                              recv_sem.at[which]).start()

    pair(1)
    exchange(res_a.at[1], got_a.at[1], 1, True)

    @pl.when(me > 0)
    def _():
        halo.wait_recv()

    for i in range(2):
        norm_act(before, i, i)
    for i in range(2):
        conv(i, i)
    pair(0)
    exchange(res_a.at[0], got_a.at[0], 0, True)
    pack = None
    for f in range(frames):
        put_at = spread(chans, 128, lambda r: over(r, gw) + f * GROUPS, lambda c: c)
        term = exact_dot(stat[f], put_at)
        pack = term if pack is None else pack + term
    sums[0:1] = jnp.sum(pack[:8], axis=0, keepdims=True)
    sums[1:2] = jnp.sum(pack[8:], axis=0, keepdims=True)
    exchange(sums, got_sums, 2, False)
    exchange(res_b, got_b, 3, True)

    block = 32
    srcs = block // frames
    side = block * part_px
    group_rows = srcs * 2 * part_px

    def place(c):
        part, rest = over(c, group_rows), left_of(c, group_rows)
        src, rest = over(rest, 2 * part_px), left_of(rest, 2 * part_px)
        f = src * frames + part * 2 + over(rest, part_px)
        return left_of(rest, part_px) * block + f

    perm = spread(side, side, lambda r: r, place).astype(jnp.bfloat16)
    f_at = lax.broadcasted_iota(jnp.int32, (total, total), 0)
    g_at = lax.broadcasted_iota(jnp.int32, (total, total), 1)
    start = jnp.zeros((total, total), jnp.int32)
    at = jnp.int32(0)
    for clip in range(lengths.shape[0]):
        start = jnp.where(at <= f_at, at, start)
        at = at + lengths[clip]
    shut[...] = jnp.where((g_at <= f_at) & (g_at >= start), 0.0, 1.0)

    pltpu.make_async_copy(got_sums, got_sums, recv_sem.at[2]).wait()
    pick = spread(total, n, lambda r: over(r, frames), lambda c: c)
    lane = spread(total, 128, lambda r: left_of(r, frames), lambda c: over(c, GROUPS))
    wide = spread(128, chans, lambda r: left_of(r, GROUPS), lambda c: over(c, gw))
    count = pixels * gw
    mu = exact_dot(exact_dot(pick, got_sums[:, 0, :]) * lane, wide) / count
    sq = exact_dot(exact_dot(pick, got_sums[:, 1, :]) * lane, wide) / count
    mean_all[...] = mu
    scale_all[...] = lax.rsqrt(sq - mu * mu + EPS) * gains[1:2, :]

    def attend(at_px, number):
        x = flat[pl.ds(at_px, number)]
        normed = ((x.astype(jnp.float32) - mean_all[...][None]) * scale_all[...][None]).astype(jnp.bfloat16)
        qkv = jnp.dot(normed.reshape(number * total, chans), w_qkv[...], preferred_element_type=jnp.float32)
        query = (qkv[:, :chans] * (1.0 / math.sqrt(chans))).astype(jnp.bfloat16).reshape(number, total, chans)
        keys = qkv[:, chans:2 * chans].astype(jnp.bfloat16).reshape(number, total, chans)
        values = qkv[:, 2 * chans:].astype(jnp.bfloat16).reshape(number, total, chans)
        closed = shut[...] > 0.5
        probs = []
        for p in range(number):
            score = lax.dot_general(query[p], keys[p], (((1,), (1,)), ((), ())),
                                    preferred_element_type=jnp.float32)
            score = jnp.where(closed, -1e30, score)
            top = jnp.max(score, axis=1, keepdims=True)
            expo = jnp.exp(score - top)
            probs.append((expo * (1.0 / jnp.sum(expo, axis=1, keepdims=True))).astype(jnp.bfloat16))
        attn = jnp.concatenate(
            [jnp.dot(probs[p], values[p], preferred_element_type=jnp.float32).astype(jnp.bfloat16)
             for p in range(number)], axis=0)
        proj = jnp.dot(attn, w_out[...], preferred_element_type=jnp.float32)
        mixed = x.astype(jnp.float32) + proj.reshape(number, total, chans)
        done[pl.ds(at_px, number)] = mixed.astype(jnp.bfloat16)
        store = pltpu.make_async_copy(done.at[pl.ds(at_px, number)], out.at[0, 0, pl.ds(at_px, number)],
                                      out_sem.at[at_px // number])
        store.start()
        return store

    def regroup(at_px, piece):
        for b in range(total // block):
            x = jnp.concatenate([piece(p, b * srcs, (b + 1) * srcs) for p in range(2)], axis=0)
            y = jnp.dot(perm, x, preferred_element_type=jnp.float32).astype(jnp.bfloat16)
            flat[at_px:at_px + part_px, b * block:(b + 1) * block, :] = y.reshape(part_px, block, chans)

    stores = []
    number = part_px // 2
    for part in range(2):
        pltpu.make_async_copy(got_a.at[part], got_a.at[part], recv_sem.at[part]).wait()
    regroup(0, lambda p, lo, hi: got_a[p, lo:hi].reshape(group_rows, chans))
    for i in range(2):
        stores.append(attend(i * number, number))
    pltpu.make_async_copy(got_b, got_b, recv_sem.at[3]).wait()
    regroup(part_px, lambda p, lo, hi: got_b[lo:hi, p * 2 * part_px:(p + 1) * 2 * part_px].reshape(group_rows, chans))
    for i in range(2):
        stores.append(attend(part_px + i * number, number))

    @pl.when(me < n - 1)
    def _():
        halo.wait_send()

    for part in range(2):
        pltpu.make_async_copy(got_a.at[part, pl.ds(0, n - 1)], got_a.at[part, pl.ds(0, n - 1)],
                              send_sem.at[part]).wait()
    pltpu.make_async_copy(got_sums.at[pl.ds(0, n - 1)], got_sums.at[pl.ds(0, n - 1)], send_sem.at[2]).wait()
    pltpu.make_async_copy(got_b.at[pl.ds(0, n - 1)], got_b.at[pl.ds(0, n - 1)], send_sem.at[3]).wait()
    for store in stores:
        store.wait()


def whole_image(video, clip_lengths, norm_gains, spatial_kernel_weight, w_time, w_qkv, w_out):
    n = lax.axis_size("tm")
    frames, height, width, chans = video.shape
    pixels = height * width
    per = pixels // n
    total = n * frames
    vmem = pl.BlockSpec(memory_space=pltpu.VMEM)
    anyw = pl.BlockSpec(memory_space=pl.ANY)
    bf16 = jnp.bfloat16
    return pl.pallas_call(
        lambda *refs: kernel(n, *refs),
        out_shape=jax.ShapeDtypeStruct((1, 1, per, total, chans), bf16),
        in_specs=[pl.BlockSpec(memory_space=pltpu.SMEM), vmem, vmem, anyw, anyw, vmem, vmem],
        out_specs=anyw,
        scratch_shapes=[
            pltpu.VMEM((2, height, width, chans), bf16),
            pltpu.VMEM((frames, height + 2, width, 3 * chans), bf16),
            pltpu.VMEM((frames + 2, pixels, chans), bf16),
            pltpu.VMEM((2, n, per, chans), bf16),
            pltpu.VMEM((n, 2 * per, chans), bf16),
            pltpu.VMEM((2, n, per, chans), bf16),
            pltpu.VMEM((n, 2 * per, chans), bf16),
            pltpu.VMEM((2, 128), jnp.float32),
            pltpu.VMEM((n, 2, 128), jnp.float32),
            pltpu.VMEM((9 * chans, chans), bf16),
            pltpu.VMEM((3 * chans, chans), bf16),
            pltpu.VMEM((per, total, chans), bf16),
            pltpu.VMEM((per, total, chans), bf16),
            pltpu.VMEM((total, chans), jnp.float32),
            pltpu.VMEM((total, chans), jnp.float32),
            pltpu.VMEM((total, total), jnp.float32),
            pltpu.SemaphoreType.DMA((12,)),
            pltpu.SemaphoreType.DMA((2,)),
            pltpu.SemaphoreType.DMA((4,)),
            pltpu.SemaphoreType.DMA((4,)),
            pltpu.SemaphoreType.DMA((4,)),
        ],
        compiler_params=pltpu.CompilerParams(
            collective_id=0, has_side_effects=True, vmem_limit_bytes=VMEM_BYTES),
        cost_estimate=pl.CostEstimate(flops=5_000_000_000, bytes_accessed=4_000_000, transcendentals=900_000),
        name="block",
    )(clip_lengths, video, norm_gains, spatial_kernel_weight, w_time, w_qkv, w_out)


def solution(mesh):
    alone = mesh.shape["band"] * mesh.shape["fsdp"] == 1
    return jax.shard_map(
        whole_image if alone else body,
        mesh=mesh,
        in_specs=(
            P("tm", "band", "fsdp", None),
            P(),
            P(),
            P(("band", "fsdp"), None),
            P(("band", "fsdp"), None),
            P(("band", "fsdp"), None),
            P(("band", "fsdp"), None),
        ),
        out_specs=P("band", "fsdp", "tm", None, None),
        check_vma=False,
    )
```
